32 devices in a mesh: groups: 2 (over x), tensor: 8 (over z, y), seq: 2 (over core).
Axes of the slice: x: 2, y: 2, z: 4, core: 2. Of those that a mesh axis runs over, the one named last changes fastest.
Arguments:
- tokens: bfloat16 [4, 256, 3584], P(('groups', 'seq'), 'tensor'), parts along dimension 0, may hold values from -2048 to 2048
- section_of_row: int32 [1024], P('groups'), parts along dimension 0, may hold values from 0 to 7, never falling along the last dimension, each value on 1 to 128 neighbouring positions
- section_kind: int32 [16], P('groups'), parts along dimension 0, may hold values 0 or 1
- norm_gain: bfloat16 [2, 3584], replicated, may hold values from 0.099609375 to 1.8984375
- qkv_weight: bfloat16 [2, 3584, 4608], P(None, None, 'tensor'), may hold values from -4 to 4
- qkv_bias: bfloat16 [2, 4608], P(None, 'tensor'), may hold values from -3 to 3
- out_weight: bfloat16 [2, 3584, 3584], P(None, 'tensor'), may hold values from -0.09375 to 0.09375
Outputs:
- attn_out: bfloat16 [4, 256, 3584], P(('groups', 'seq'), 'tensor'), parts along dimension 0
The draws below stay inside these ranges and needn't reach their ends.
There are 2 independent parts, one for each index of `groups`. The reference program is written for one: setup_inputs(seed, part) draws one part's arguments, and reference() takes and returns one part's arrays. A program takes and returns all parts, laid end to end along the dimension named above; an argument that names none is the same for every part. Nothing has to cross between parts.
Inputs may be any that keep to these rules, and one draw needn't show every extreme that they name: `section_of_row`: section numbers never fall along the rows; each section holds 1 to 128 rows and one holds exactly 128. `section_kind`: 1 marks an image section, 0 a text section.
All inputs are finite; a program needn't handle non-finite values.
Results may differ from the reference program's by a relative error of at most 0.024.
Values may be sent and summed in bfloat16 or wider, within the bound.
A program may use at most 64 MiB of HBM per device.

```python
import math
import jax
import jax.numpy as jnp
import numpy as np
from jax import lax

MODEL_WIDTH = 3584
QUERY_HEADS = 28
KEY_VALUE_HEADS = 4
HEAD_SIZE = 128
SECTIONS = 8
QKV_COLS = 4608
GROUP_ROWS = 256
SEQUENCE_ROWS = 512
SEC_MOST = 128
N_SEQ = 2


def draw_tokens(key, part):
    random_subkeys = jax.random.split(key, 4)
    column_index = jnp.arange(MODEL_WIDTH, dtype=jnp.float32) / MODEL_WIDTH
    column_spread = jnp.exp(jax.random.uniform(random_subkeys[1], (MODEL_WIDTH,), jnp.float32, 0.0, math.log(10.0)))
    starting_sample = jnp.clip(jax.random.normal(random_subkeys[0], (SEQUENCE_ROWS, MODEL_WIDTH), jnp.float32), -5.0, 5.0)
    row_spread = jnp.exp(jax.random.uniform(random_subkeys[3], (SEQUENCE_ROWS, 1), jnp.float32, 0.0, math.log(10.0)))
    value_matrix = starting_sample * 3.0 ** column_index * column_spread * row_spread
    value_matrix = jnp.clip(value_matrix, -2048.0, 2048.0)
    return value_matrix.reshape(SEQUENCE_ROWS // GROUP_ROWS, GROUP_ROWS, MODEL_WIDTH).astype(jnp.bfloat16)


def draw_qkv_weight(key, part):
    random_subkeys = jax.random.split(key, 2)
    input_scale = 1.0 / math.sqrt(MODEL_WIDTH)
    starting_sample = jnp.clip(jax.random.normal(random_subkeys[0], (2, MODEL_WIDTH, QKV_COLS), jnp.float32), -4.0, 4.0) * input_scale
    weight_magnitude = jnp.exp(jax.random.uniform(random_subkeys[1], (2, 1, QUERY_HEADS, 1), jnp.float32, math.log(1.5), math.log(3.0)))
    query_portion = starting_sample[:, :, :QUERY_HEADS * HEAD_SIZE].reshape(2, MODEL_WIDTH, QUERY_HEADS, HEAD_SIZE) * weight_magnitude
    key_portion = starting_sample[:, :, QUERY_HEADS * HEAD_SIZE:(QUERY_HEADS + KEY_VALUE_HEADS) * HEAD_SIZE]
    value_portion = starting_sample[:, :, (QUERY_HEADS + KEY_VALUE_HEADS) * HEAD_SIZE:]
    merged_result = jnp.concatenate([query_portion.reshape(2, MODEL_WIDTH, QUERY_HEADS * HEAD_SIZE), key_portion.reshape(2, MODEL_WIDTH, KEY_VALUE_HEADS * HEAD_SIZE), value_portion], axis=2)
    return jnp.clip(merged_result, -4.0, 4.0).astype(jnp.bfloat16)


def set_ends(values, stream_key, smallest, largest):
    longest = values.shape.index(max(values.shape))
    spots = []
    for shift in (0, 1):
        where = [jax.random.randint(jax.random.fold_in(stream_key, axis), (), 0, length) for axis, length in enumerate(values.shape)]
        where[longest] = (where[longest] + shift) % values.shape[longest]
        spots.append(tuple(where))
    return values.at[spots[0]].set(smallest).at[spots[1]].set(largest)


def steps_of(stream_key, extent, pieces, least, largest):
    factor_of, own = 1.0, jax.random.fold_in(stream_key, 6)
    for axis_at, shards_of in pieces:
        steps = jnp.exp(jax.random.uniform(jax.random.fold_in(own, axis_at), (shards_of,), jnp.float32, least / len(pieces), largest / len(pieces)))
        factor_of = factor_of * jnp.repeat(steps, extent[axis_at] // shards_of).reshape([-1 if axis == axis_at else 1 for axis in range(len(extent))])
    return factor_of


def length_profile(count, total, bound, skew):
    weights = [(1 << 20) // math.isqrt(standing ** skew) + 1 for standing in range(2, count + 1)]
    spare, given = total - bound - (count - 1), [1] * (count - 1)
    while spare > 0:
        movable = [i for i in range(count - 1) if given[i] < bound]
        whole, budget = sum([weights[i] for i in movable]), spare
        for i in movable:
            more = min(bound - given[i], max(1, budget * weights[i] // whole), spare)
            given[i] = given[i] + more
            spare = spare - more
    return np.array([bound] + given)


def ragged(rng, number_of, total, reach, skew):
    if number_of == 2:
        one = jax.random.randint(rng, (), max(1, total - reach), min(reach, total - 1) + 1)
        return jnp.stack([one, total - one])
    lengths = jnp.asarray(length_profile(number_of, total, reach, skew), jnp.int32)
    couples = (number_of - 1) // 2
    donor, taker = lengths[1:1 + 2 * couples:2], lengths[2:2 + 2 * couples:2]
    room = jnp.minimum(donor - 1, reach - taker)
    shifted = jax.random.randint(jax.random.fold_in(rng, 1), (couples,), 0, 1 << 20) % (room + 1)
    lengths = lengths.at[1:1 + 2 * couples:2].set(donor - shifted).at[2:2 + 2 * couples:2].set(taker + shifted)
    return lengths[jax.random.permutation(jax.random.fold_in(rng, 2), number_of)]


def noise(key, shape, scale, bound, cuts=(), kind=jnp.bfloat16):
    level = steps_of(key, shape, cuts, -0.22, 0.18) if cuts else 1.0
    values = jax.random.normal(key, shape, jnp.float32) * scale * level
    return jnp.minimum(jnp.maximum(values, -bound), bound).astype(kind)


def setup_inputs(seed: int = 0, part: int = 0) -> dict:
    streams_of = jax.random.split(jax.random.key(seed), 8)
    own_keys = jax.random.split(jax.random.fold_in(streams_of[7], part), 8)
    return {
        "tokens": draw_tokens(jax.random.fold_in(jax.random.fold_in(streams_of[7], part), 71), part),
        "section_of_row": jnp.searchsorted(jnp.cumsum(ragged(own_keys[1], SECTIONS, SEQUENCE_ROWS, SEC_MOST, 1)), jnp.arange(SEQUENCE_ROWS), side="right").astype(jnp.int32),
        "section_kind": set_ends((jax.random.randint(own_keys[2], (SECTIONS,), 0, 2) < 1).astype(jnp.int32), jax.random.fold_in(own_keys[2], 1), 0, 1),
        "norm_gain": jnp.clip(1.0 + 0.18 * jax.random.normal(streams_of[3], (2, MODEL_WIDTH), jnp.float32), 0.099609375, 1.8984375).astype(jnp.bfloat16),
        "qkv_weight": draw_qkv_weight(jax.random.fold_in(streams_of[7], 71), part),
        "qkv_bias": noise(streams_of[5], (2, QKV_COLS), 0.5, 3.0, ((1, 8),)),
        "out_weight": noise(streams_of[6], (2, QUERY_HEADS * HEAD_SIZE, MODEL_WIDTH), (QUERY_HEADS * HEAD_SIZE) ** -0.5, 0.09375, ((1, 8),)),
    }


NORM_EPSILON = 1e-06
ROPE_THETA = 1000000.0

def apply_rotation(value_matrix, token_places, head_count):
    row_count = value_matrix.shape[0]
    head_dim = value_matrix.shape[1] // head_count
    field_rows = value_matrix.astype(jnp.float32).reshape(row_count, head_count, head_dim)
    frequencies = ROPE_THETA ** (-(jnp.arange(0, head_dim, 2, dtype=jnp.float32) / head_dim))
    angles = token_places.astype(jnp.float32)[:, None] * frequencies[None, :]
    angles = jnp.concatenate([angles, angles], axis=1)
    cosine = jnp.cos(angles)[:, None, :]
    sine_part = jnp.sin(angles)[:, None, :]
    first_half = field_rows[:, :, :head_dim // 2]
    second_half = field_rows[:, :, head_dim // 2:]
    turned = jnp.concatenate([-second_half, first_half], axis=2)
    rotated = field_rows * cosine + turned * sine_part
    return rotated.reshape(row_count, head_count * head_dim).astype(jnp.bfloat16)

def reference(tokens, section_of_row, section_kind, norm_gain, qkv_weight, qkv_bias, out_weight):
    features = tokens.reshape(SEQUENCE_ROWS, MODEL_WIDTH).astype(jnp.float32)
    labels = jnp.arange(SECTIONS, dtype=jnp.int32)
    kind_rows = lax.optimization_barrier(jnp.sum(jnp.where(section_of_row[:, None] == labels[None, :], section_kind[None, :], 0), axis=1))
    image_rows = kind_rows == 1
    gain_rows = jnp.where(image_rows[:, None], norm_gain[1], norm_gain[0]).astype(jnp.float32)
    scaled = lax.rsqrt(lax.optimization_barrier(jnp.mean(features * features, axis=1, keepdims=True)) + NORM_EPSILON)
    normed = (features * scaled * gain_rows).astype(jnp.bfloat16)
    text_qkv = jnp.dot(normed, qkv_weight[0], preferred_element_type=jnp.float32) + qkv_bias[0].astype(jnp.float32)
    image_qkv = jnp.dot(normed, qkv_weight[1], preferred_element_type=jnp.float32) + qkv_bias[1].astype(jnp.float32)
    projected_rows = jnp.where(image_rows[:, None], image_qkv, text_qkv).astype(jnp.bfloat16)
    projected_rows = lax.optimization_barrier(projected_rows)
    token_places = jnp.arange(SEQUENCE_ROWS, dtype=jnp.int32)
    query_matrix = apply_rotation(projected_rows[:, :QUERY_HEADS * HEAD_SIZE], token_places, QUERY_HEADS)
    key_row_values = apply_rotation(projected_rows[:, QUERY_HEADS * HEAD_SIZE:(QUERY_HEADS + KEY_VALUE_HEADS) * HEAD_SIZE], token_places, KEY_VALUE_HEADS)
    value_matrix = projected_rows[:, (QUERY_HEADS + KEY_VALUE_HEADS) * HEAD_SIZE:]
    query_matrix, key_row_values = lax.optimization_barrier((query_matrix, key_row_values))
    queries_per_group = QUERY_HEADS // KEY_VALUE_HEADS
    key_head_tensor = jnp.repeat(key_row_values.astype(jnp.float32).reshape(SEQUENCE_ROWS, KEY_VALUE_HEADS, HEAD_SIZE), queries_per_group, axis=1)
    value_head_tensor = jnp.repeat(value_matrix.astype(jnp.float32).reshape(SEQUENCE_ROWS, KEY_VALUE_HEADS, HEAD_SIZE), queries_per_group, axis=1)
    block_rows = math.gcd(SEQUENCE_ROWS, 128)
    block_count = SEQUENCE_ROWS // block_rows
    query_heads = query_matrix.astype(jnp.float32).reshape(block_count, block_rows, QUERY_HEADS, HEAD_SIZE)

    def attend(block):
        query_block, block_pos, block_sec, block_img = block
        scores = jnp.einsum('qha,kha->hqk', query_block, key_head_tensor) / math.sqrt(HEAD_SIZE)
        allowed = (token_places[None, :] <= block_pos[:, None]) | (section_of_row[None, :] == block_sec[:, None]) & block_img[:, None]
        scores = jnp.where(allowed[None], scores, -jnp.inf)
        row_max = lax.optimization_barrier(jnp.max(scores, axis=2, keepdims=True))
        weights = jnp.where(allowed[None], jnp.exp(scores - row_max), 0.0)
        row_total = lax.optimization_barrier(jnp.sum(weights, axis=2))
        rounded = lax.optimization_barrier(weights.astype(jnp.bfloat16)).astype(jnp.float32)
        summed = jnp.einsum('hqk,kha->qha', rounded, value_head_tensor)
        return (summed / jnp.transpose(row_total)[:, :, None]).astype(jnp.bfloat16)
    attention_result = lax.map(attend, (query_heads, token_places.reshape(block_count, block_rows), section_of_row.reshape(block_count, block_rows), image_rows.reshape(block_count, block_rows)))
    attention_result = attention_result.reshape(SEQUENCE_ROWS, QUERY_HEADS * HEAD_SIZE)
    text_out = jnp.dot(attention_result, out_weight[0], preferred_element_type=jnp.float32)
    image_out = jnp.dot(attention_result, out_weight[1], preferred_element_type=jnp.float32)
    merged_result = jnp.where(image_rows[:, None], image_out, text_out).astype(jnp.bfloat16)
    return merged_result.reshape(N_SEQ, GROUP_ROWS, MODEL_WIDTH)
```

```python
import math

import jax
import jax.numpy as jnp
from jax import lax
from jax.sharding import PartitionSpec as P

QUERY_HEADS = 28
KEY_VALUE_HEADS = 4
HEAD_SIZE = 128


NORM_EPSILON = 1e-06
ROPE_THETA = 1000000.0
BLOCKED_SCORE = -1e30


def row_kinds(section_of_row, section_kind):
    labels = jnp.arange(section_kind.shape[0], dtype=jnp.int32)
    matches = section_of_row[:, None] == labels[None, :]
    return jnp.sum(jnp.where(matches, section_kind[None, :], 0), axis=1)


def apply_rotation(value_matrix, token_places, head_count):
    row_count = value_matrix.shape[0]
    head_dim = value_matrix.shape[1] // head_count
    field_rows = value_matrix.astype(jnp.float32).reshape(row_count, head_count, head_dim)
    frequencies = ROPE_THETA ** (-(jnp.arange(0, head_dim, 2, dtype=jnp.float32) / head_dim))
    angles = token_places.astype(jnp.float32)[:, None] * frequencies[None, :]
    angles = jnp.concatenate([angles, angles], axis=1)
    cosine = jnp.cos(angles)[:, None, :]
    sine_part = jnp.sin(angles)[:, None, :]
    first_half = field_rows[:, :, : head_dim // 2]
    second_half = field_rows[:, :, head_dim // 2 :]
    turned = jnp.concatenate([-second_half, first_half], axis=2)
    rotated = field_rows * cosine + turned * sine_part
    return rotated.reshape(row_count, head_count * head_dim).astype(jnp.bfloat16)


def both_kinds(row_slab, weights, kind_rows):
    first_kind = jnp.dot(row_slab, weights[0], preferred_element_type=jnp.float32)
    second_kind = jnp.dot(row_slab, weights[1], preferred_element_type=jnp.float32)
    return jnp.where(kind_rows[:, None] == 1, second_kind, first_kind)


def project_rows(row_slab, weights, kind_rows):
    return both_kinds(row_slab, weights, kind_rows)


def body(tokens, section_of_row, section_kind, norm_gain, qkv_weight, qkv_bias, out_weight):
    tensor_size = lax.axis_size("tensor")
    tensor_rank = lax.axis_index("tensor")
    seq_rank = lax.axis_index("seq")
    own_rows = tokens.shape[1]
    group_rows = own_rows * tensor_size
    query_span_width = QUERY_HEADS * HEAD_SIZE
    key_value_width = KEY_VALUE_HEADS * HEAD_SIZE
    queries_per_group = QUERY_HEADS // KEY_VALUE_HEADS
    kinds_all = row_kinds(section_of_row, section_kind)
    group_start = seq_rank * group_rows
    kinds_group = lax.dynamic_slice_in_dim(kinds_all, group_start, group_rows)
    own_kinds = lax.dynamic_slice_in_dim(kinds_group, tensor_rank * own_rows, own_rows)
    features = tokens[0].astype(jnp.float32)
    gain_rows = jnp.where(own_kinds[:, None] == 1, norm_gain[1], norm_gain[0]).astype(jnp.float32)
    scaled = lax.rsqrt(jnp.mean(features * features, axis=1, keepdims=True) + NORM_EPSILON)
    normed = (features * scaled * gain_rows).astype(jnp.bfloat16)
    bias_pair = qkv_bias.astype(jnp.float32)
    product = project_rows(
        lax.all_gather(normed, "tensor", axis=0, tiled=True), qkv_weight, kinds_group
    )
    column_block = (
        product + jnp.where(kinds_group[:, None] == 1, bias_pair[1], bias_pair[0])
    ).astype(jnp.bfloat16)
    iota_own = jnp.arange(own_rows, dtype=jnp.int32)
    key_places = group_start + tensor_rank * own_rows + iota_own
    row_tile = lax.all_to_all(column_block, "tensor", split_axis=0, concat_axis=1, tiled=True)
    query_matrix = apply_rotation(row_tile[:, :query_span_width], key_places, QUERY_HEADS)
    key_row_values = apply_rotation(
        row_tile[:, query_span_width : query_span_width + key_value_width],
        key_places,
        KEY_VALUE_HEADS,
    )
    value_matrix = row_tile[:, query_span_width + key_value_width :]
    slab = lax.all_gather(
        jnp.concatenate([key_row_values, value_matrix], axis=1), ("tensor", "seq"), axis=0, tiled=True
    )
    seq_size = lax.axis_size("seq")
    total_keys = own_rows * tensor_size * seq_size
    sections_grid = section_of_row.reshape(seq_size, tensor_size, own_rows)
    key_sections = sections_grid.transpose(1, 0, 2).reshape(total_keys)
    key_pos = (
        jnp.arange(total_keys, dtype=jnp.int32)
        .reshape(seq_size, tensor_size, own_rows)
        .transpose(1, 0, 2)
        .reshape(total_keys)
    )
    query_sections = lax.dynamic_slice_in_dim(
        section_of_row, group_start + tensor_rank * own_rows, own_rows
    )
    query_image = own_kinds == 1
    allowed = (key_pos[None, :] <= key_places[:, None]) | (
        key_sections[None, :] == query_sections[:, None]
    ) & query_image[:, None]
    grouped_queries = query_matrix.reshape(own_rows, KEY_VALUE_HEADS, queries_per_group, HEAD_SIZE)
    grouped_queries = grouped_queries.transpose(1, 2, 0, 3).reshape(
        KEY_VALUE_HEADS, queries_per_group * own_rows, HEAD_SIZE
    )
    key_heads = slab[:, :key_value_width].reshape(total_keys, KEY_VALUE_HEADS, HEAD_SIZE)
    value_heads = slab[:, key_value_width:].reshape(total_keys, KEY_VALUE_HEADS, HEAD_SIZE)
    scores = jnp.einsum(
        "gqa,kga->gqk", grouped_queries, key_heads, preferred_element_type=jnp.float32
    ) * (1.0 / math.sqrt(HEAD_SIZE))
    allowed = jnp.broadcast_to(
        allowed[None, None], (1, queries_per_group, own_rows, total_keys)
    ).reshape(1, queries_per_group * own_rows, total_keys)
    scores = jnp.where(allowed, scores, BLOCKED_SCORE)
    peak = jnp.max(scores, axis=2, keepdims=True)
    weights = jnp.where(allowed, jnp.exp(scores - peak), 0.0)
    total = jnp.sum(weights, axis=2)
    summed = jnp.einsum(
        "gqk,kga->gqa",
        weights.astype(jnp.bfloat16),
        value_heads,
        preferred_element_type=jnp.float32,
    )
    attention_result = (summed / total[:, :, None]).astype(jnp.bfloat16)
    attention_result = (
        attention_result.reshape(KEY_VALUE_HEADS, queries_per_group, own_rows, HEAD_SIZE)
        .transpose(2, 0, 1, 3)
        .reshape(own_rows, query_span_width)
    )
    head_block = lax.all_to_all(attention_result, "tensor", split_axis=1, concat_axis=0, tiled=True)
    result = lax.psum_scatter(
        project_rows(head_block, out_weight, kinds_group).astype(jnp.bfloat16),
        "tensor",
        scatter_dimension=0,
        tiled=True,
    )
    return result[None]


def solution(mesh):
    placed = (
        P(("groups", "seq"), "tensor", None),
        P("groups"),
        P("groups"),
        P(),
        P(None, None, "tensor"),
        P(None, "tensor"),
        P(None, "tensor", None),
    )
    return jax.shard_map(
        body,
        mesh=mesh,
        in_specs=placed,
        out_specs=P(("groups", "seq"), "tensor", None),
        check_vma=False,
    )
```

```python
import functools
import math

import jax
import jax.numpy as jnp
from jax import lax
from jax.experimental import pallas as pl
from jax.experimental.pallas import tpu as pltpu
from jax.sharding import PartitionSpec as P

QUERY_HEADS = 28
KEY_VALUE_HEADS = 4
HEAD_SIZE = 128


NORM_EPSILON = 1e-06
ROPE_THETA = 1000000.0
BLOCKED_SCORE = -1e30


MESH_ID = pl.DeviceIdType.MESH


def greet(peers):
    barrier = pltpu.get_barrier_semaphore()
    for peer in peers:
        pl.semaphore_signal(barrier, inc=1, device_id=peer, device_id_type=MESH_ID)
    pl.semaphore_wait(barrier, len(peers))


def gather_kernel(n, across, x_ref, out_ref, line_send, line_recv, pair_send, pair_recv, seq_send, seq_recv):
    rank = lax.axis_index("tensor")
    half = n // 2
    high, low = rank // 2, rank % 2
    slab = lax.axis_index("seq") if across else 0
    pair = {"tensor": high * 2 + 1 - low}
    line = [{"tensor": ((high + d) % half) * 2 + low} for d in range(1, half)]
    other = {"seq": 1 - lax.axis_index("seq")}
    greet(line + [pair] + ([other] if across else []))

    def push(src, block, send, recv, to):
        copy = pltpu.make_async_remote_copy(
            src_ref=src,
            dst_ref=out_ref.at[slab, block],
            send_sem=send,
            recv_sem=recv,
            device_id=to,
            device_id_type=MESH_ID,
        )
        copy.start()
        return copy

    lines = [push(x_ref, rank, line_send.at[d], line_recv.at[d], line[d]) for d in range(half - 1)]
    pairs = [push(x_ref, rank, pair_send.at[half - 1], pair_recv.at[half - 1], pair)]
    crossed = []
    if across:
        crossed.append(push(x_ref, rank, seq_send.at[n - 1], seq_recv.at[n - 1], other))
    out_ref[slab, rank] = x_ref[...]
    for d in range(half - 1):
        lines[d].wait_recv()
        block = ((high + half - d - 1) % half) * 2 + low
        pairs.append(push(out_ref.at[slab, block], block, pair_send.at[d], pair_recv.at[d], pair))
        if across:
            crossed.append(
                push(out_ref.at[slab, block], block, seq_send.at[d], seq_recv.at[d], other)
            )
    for d in range(half):
        pairs[d].wait_recv()
        if across:
            block = ((high + half - d) % half) * 2 + 1 - low
            at = half - 1 + d
            crossed.append(
                push(out_ref.at[slab, block], block, seq_send.at[at], seq_recv.at[at], other)
            )
    for copy in crossed:
        copy.wait_recv()
    for copy in lines + pairs + crossed:
        copy.wait_send()


def gather_rows(block, n, across, name_id):
    rows, columns = block.shape
    slabs = 2 if across else 1
    return pl.pallas_call(
        functools.partial(gather_kernel, n, across),
        out_shape=jax.ShapeDtypeStruct((slabs, n, rows, columns), block.dtype),
        in_specs=[pl.BlockSpec(memory_space=pltpu.VMEM)],
        out_specs=pl.BlockSpec(memory_space=pltpu.VMEM),
        scratch_shapes=[
            pltpu.SemaphoreType.DMA((n // 2,)),
            pltpu.SemaphoreType.DMA((n // 2,)),
            pltpu.SemaphoreType.DMA((n // 2,)),
            pltpu.SemaphoreType.DMA((n // 2,)),
            pltpu.SemaphoreType.DMA((n,)),
            pltpu.SemaphoreType.DMA((n,)),
        ],
        compiler_params=pltpu.CompilerParams(collective_id=name_id, has_side_effects=True),
    )(block).reshape(slabs * n * rows, columns)


def scatter_kernel(
    n, p_ref, out_ref, stage, from_pair, from_line, pair_send, pair_recv, line_send, line_recv
):
    rank = lax.axis_index("tensor")
    half = n // 2
    high, low = rank // 2, rank % 2
    pair = {"tensor": high * 2 + 1 - low}
    line = [{"tensor": ((high + d) % half) * 2 + low} for d in range(1, half)]
    greet(line + [pair])
    order = list(range(1, half)) + [0]
    pairs = {}
    for d in order:
        pairs[d] = pltpu.make_async_remote_copy(
            src_ref=p_ref.at[((high + d) % half) * 2 + 1 - low],
            dst_ref=from_pair.at[d],
            send_sem=pair_send.at[d],
            recv_sem=pair_recv.at[d],
            device_id=pair,
            device_id_type=MESH_ID,
        )
        pairs[d].start()
    columns = p_ref.shape[2]
    lines = []
    for d in order:
        pairs[d].wait_recv()
        mine = ((high + d) % half) * 2 + low
        if d:
            for c in range(0, columns, 512):
                both = p_ref[mine, :, c : c + 512].astype(jnp.float32) + from_pair[
                    d, :, c : c + 512
                ].astype(jnp.float32)
                stage[d - 1, :, c : c + 512] = both.astype(jnp.bfloat16)
            copy = pltpu.make_async_remote_copy(
                src_ref=stage.at[d - 1],
                dst_ref=from_line.at[d - 1],
                send_sem=line_send.at[d - 1],
                recv_sem=line_recv.at[d - 1],
                device_id=line[d - 1],
                device_id_type=MESH_ID,
            )
            copy.start()
            lines.append(copy)
    for copy in lines:
        copy.wait_recv()
    for c in range(0, columns, 512):
        both = p_ref[rank, :, c : c + 512].astype(jnp.float32) + from_pair[
            0, :, c : c + 512
        ].astype(jnp.float32)
        for d in range(half - 1):
            both = both + from_line[d, :, c : c + 512].astype(jnp.float32)
        out_ref[:, c : c + 512] = both.astype(jnp.bfloat16)
    for d in order:
        pairs[d].wait_send()
    for copy in lines:
        copy.wait_send()


def scatter_sums(partial, n):
    rows, columns = partial.shape[0] // n, partial.shape[1]
    half = n // 2
    return pl.pallas_call(
        functools.partial(scatter_kernel, n),
        out_shape=jax.ShapeDtypeStruct((rows, columns), partial.dtype),
        in_specs=[pl.BlockSpec(memory_space=pltpu.VMEM)],
        out_specs=pl.BlockSpec(memory_space=pltpu.VMEM),
        scratch_shapes=[
            pltpu.VMEM((half - 1, rows, columns), jnp.bfloat16),
            pltpu.VMEM((half, rows, columns), jnp.bfloat16),
            pltpu.VMEM((half - 1, rows, columns), jnp.bfloat16),
            pltpu.SemaphoreType.DMA((half,)),
            pltpu.SemaphoreType.DMA((half,)),
            pltpu.SemaphoreType.DMA((half,)),
            pltpu.SemaphoreType.DMA((half,)),
        ],
        compiler_params=pltpu.CompilerParams(
            collective_id=2, has_side_effects=True, vmem_limit_bytes=32 * 1024 * 1024
        ),
    )(partial.reshape(n, rows, columns))


def row_kinds(section_of_row, section_kind):
    labels = jnp.arange(section_kind.shape[0], dtype=jnp.int32)
    matches = section_of_row[:, None] == labels[None, :]
    return jnp.sum(jnp.where(matches, section_kind[None, :], 0), axis=1)


def apply_rotation(value_matrix, token_places, head_count):
    row_count = value_matrix.shape[0]
    head_dim = value_matrix.shape[1] // head_count
    field_rows = value_matrix.astype(jnp.float32).reshape(row_count, head_count, head_dim)
    frequencies = ROPE_THETA ** (-(jnp.arange(0, head_dim, 2, dtype=jnp.float32) / head_dim))
    angles = token_places.astype(jnp.float32)[:, None] * frequencies[None, :]
    angles = jnp.concatenate([angles, angles], axis=1)
    cosine = jnp.cos(angles)[:, None, :]
    sine_part = jnp.sin(angles)[:, None, :]
    first_half = field_rows[:, :, : head_dim // 2]
    second_half = field_rows[:, :, head_dim // 2 :]
    turned = jnp.concatenate([-second_half, first_half], axis=2)
    rotated = field_rows * cosine + turned * sine_part
    return rotated.reshape(row_count, head_count * head_dim).astype(jnp.bfloat16)


def both_kinds(row_slab, weights, kind_rows):
    first_kind = jnp.dot(row_slab, weights[0], preferred_element_type=jnp.float32)
    second_kind = jnp.dot(row_slab, weights[1], preferred_element_type=jnp.float32)
    return jnp.where(kind_rows[:, None] == 1, second_kind, first_kind)


def project_rows(row_slab, weights, kind_rows):
    return both_kinds(row_slab, weights, kind_rows)


def body(tokens, section_of_row, section_kind, norm_gain, qkv_weight, qkv_bias, out_weight):
    tensor_size = lax.axis_size("tensor")
    tensor_rank = lax.axis_index("tensor")
    seq_rank = lax.axis_index("seq")
    own_rows = tokens.shape[1]
    group_rows = own_rows * tensor_size
    query_span_width = QUERY_HEADS * HEAD_SIZE
    key_value_width = KEY_VALUE_HEADS * HEAD_SIZE
    queries_per_group = QUERY_HEADS // KEY_VALUE_HEADS
    kinds_all = row_kinds(section_of_row, section_kind)
    group_start = seq_rank * group_rows
    kinds_group = lax.dynamic_slice_in_dim(kinds_all, group_start, group_rows)
    own_kinds = lax.dynamic_slice_in_dim(kinds_group, tensor_rank * own_rows, own_rows)
    features = tokens[0].astype(jnp.float32)
    gain_rows = jnp.where(own_kinds[:, None] == 1, norm_gain[1], norm_gain[0]).astype(jnp.float32)
    scaled = lax.rsqrt(jnp.mean(features * features, axis=1, keepdims=True) + NORM_EPSILON)
    normed = (features * scaled * gain_rows).astype(jnp.bfloat16)
    bias_pair = qkv_bias.astype(jnp.float32)
    product = project_rows(
        gather_rows(normed, tensor_size, False, 0), qkv_weight, kinds_group
    )
    column_block = (
        product + jnp.where(kinds_group[:, None] == 1, bias_pair[1], bias_pair[0])
    ).astype(jnp.bfloat16)
    iota_own = jnp.arange(own_rows, dtype=jnp.int32)
    key_places = group_start + tensor_rank * own_rows + iota_own
    row_tile = lax.all_to_all(column_block, "tensor", split_axis=0, concat_axis=1, tiled=True)
    query_matrix = apply_rotation(row_tile[:, :query_span_width], key_places, QUERY_HEADS)
    key_row_values = apply_rotation(
        row_tile[:, query_span_width : query_span_width + key_value_width],
        key_places,
        KEY_VALUE_HEADS,
    )
    value_matrix = row_tile[:, query_span_width + key_value_width :]
    slab = gather_rows(
        jnp.concatenate([key_row_values, value_matrix], axis=1), tensor_size, True, 1
    )
    total_keys = slab.shape[0]
    key_sections = section_of_row
    key_pos = jnp.arange(total_keys, dtype=jnp.int32)
    query_sections = lax.dynamic_slice_in_dim(
        section_of_row, group_start + tensor_rank * own_rows, own_rows
    )
    query_image = own_kinds == 1
    allowed = (key_pos[None, :] <= key_places[:, None]) | (
        key_sections[None, :] == query_sections[:, None]
    ) & query_image[:, None]
    grouped_queries = query_matrix.reshape(own_rows, KEY_VALUE_HEADS, queries_per_group, HEAD_SIZE)
    grouped_queries = grouped_queries.transpose(1, 2, 0, 3).reshape(
        KEY_VALUE_HEADS, queries_per_group * own_rows, HEAD_SIZE
    )
    key_heads = slab[:, :key_value_width].reshape(total_keys, KEY_VALUE_HEADS, HEAD_SIZE)
    value_heads = slab[:, key_value_width:].reshape(total_keys, KEY_VALUE_HEADS, HEAD_SIZE)
    scores = jnp.einsum(
        "gqa,kga->gqk", grouped_queries, key_heads, preferred_element_type=jnp.float32
    ) * (1.0 / math.sqrt(HEAD_SIZE))
    allowed = jnp.broadcast_to(
        allowed[None, None], (1, queries_per_group, own_rows, total_keys)
    ).reshape(1, queries_per_group * own_rows, total_keys)
    scores = jnp.where(allowed, scores, BLOCKED_SCORE)
    peak = jnp.max(scores, axis=2, keepdims=True)
    weights = jnp.where(allowed, jnp.exp(scores - peak), 0.0)
    total = jnp.sum(weights, axis=2)
    summed = jnp.einsum(
        "gqk,kga->gqa",
        weights.astype(jnp.bfloat16),
        value_heads,
        preferred_element_type=jnp.float32,
    )
    attention_result = (summed / total[:, :, None]).astype(jnp.bfloat16)
    attention_result = (
        attention_result.reshape(KEY_VALUE_HEADS, queries_per_group, own_rows, HEAD_SIZE)
        .transpose(2, 0, 1, 3)
        .reshape(own_rows, query_span_width)
    )
    head_block = lax.all_to_all(attention_result, "tensor", split_axis=1, concat_axis=0, tiled=True)
    result = scatter_sums(
        project_rows(head_block, out_weight, kinds_group).astype(jnp.bfloat16), tensor_size
    )
    return result[None]


def solution(mesh):
    placed = (
        P(("groups", "seq"), "tensor", None),
        P("groups"),
        P("groups"),
        P(),
        P(None, None, "tensor"),
        P(None, "tensor"),
        P(None, "tensor", None),
    )
    return jax.shard_map(
        body,
        mesh=mesh,
        in_specs=placed,
        out_specs=P(("groups", "seq"), "tensor", None),
        check_vma=False,
    )
```

```python
import functools
import math

import jax
import jax.numpy as jnp
from jax import lax
from jax.experimental import pallas as pl
from jax.experimental.pallas import tpu as pltpu
from jax.sharding import PartitionSpec as P

QUERY_HEADS = 28
KEY_VALUE_HEADS = 4
HEAD_SIZE = 128


NORM_EPSILON = 1e-06
ROPE_THETA = 1000000.0
BLOCKED_SCORE = -1e30


MESH_ID = pl.DeviceIdType.MESH
PIECES = 2


def greet(peers):
    barrier = pltpu.get_barrier_semaphore()
    for peer in peers:
        pl.semaphore_signal(barrier, inc=1, device_id=peer, device_id_type=MESH_ID)
    pl.semaphore_wait(barrier, len(peers))


def gather_kernel(n, across, x_ref, out_ref, line_send, line_recv, pair_send, pair_recv, seq_send, seq_recv):
    rank = lax.axis_index("tensor")
    half = n // 2
    high, low = rank // 2, rank % 2
    slab = lax.axis_index("seq") if across else 0
    pair = {"tensor": high * 2 + 1 - low}
    line = [{"tensor": ((high + d) % half) * 2 + low} for d in range(1, half)]
    other = {"seq": 1 - lax.axis_index("seq")}
    greet(line + [pair] + ([other] if across else []))

    rows = x_ref.shape[0] // PIECES

    def push(own, block, piece, sends, recvs, at, to):
        span = pl.ds(piece * rows, rows)
        spot = at * PIECES + piece
        copy = pltpu.make_async_remote_copy(
            src_ref=x_ref.at[span] if own else out_ref.at[slab, block, span],
            dst_ref=out_ref.at[slab, block, span],
            send_sem=sends.at[spot],
            recv_sem=recvs.at[spot],
            device_id=to,
            device_id_type=MESH_ID,
        )
        copy.start()
        return copy

    lines, pairs, crossed = [], [], []
    for c in range(PIECES):
        for d in range(half - 1):
            lines.append(push(True, rank, c, line_send, line_recv, d, line[d]))
        pairs.append(push(True, rank, c, pair_send, pair_recv, half - 1, pair))
        if across:
            crossed.append(push(True, rank, c, seq_send, seq_recv, n - 1, other))
    out_ref[slab, rank] = x_ref[...]
    for c in range(PIECES):
        for d in range(half - 1):
            lines[c * (half - 1) + d].wait_recv()
            block = ((high + half - d - 1) % half) * 2 + low
            pairs.append(push(False, block, c, pair_send, pair_recv, d, pair))
            if across:
                crossed.append(push(False, block, c, seq_send, seq_recv, d, other))
    for i in range(half):
        for c in range(PIECES):
            at = c if i == 0 else PIECES + c * (half - 1) + i - 1
            pairs[at].wait_recv()
            if across:
                block = ((high + half - i) % half) * 2 + 1 - low
                crossed.append(push(False, block, c, seq_send, seq_recv, half - 1 + i, other))
    for copy in crossed:
        copy.wait_recv()
    for copy in lines + pairs + crossed:
        copy.wait_send()


def gather_rows(block, n, across, name_id):
    rows, columns = block.shape
    slabs = 2 if across else 1
    return pl.pallas_call(
        functools.partial(gather_kernel, n, across),
        out_shape=jax.ShapeDtypeStruct((slabs, n, rows, columns), block.dtype),
        in_specs=[pl.BlockSpec(memory_space=pltpu.VMEM)],
        out_specs=pl.BlockSpec(memory_space=pltpu.VMEM),
        scratch_shapes=[
            pltpu.SemaphoreType.DMA((n // 2 * PIECES,)),
            pltpu.SemaphoreType.DMA((n // 2 * PIECES,)),
            pltpu.SemaphoreType.DMA((n // 2 * PIECES,)),
            pltpu.SemaphoreType.DMA((n // 2 * PIECES,)),
            pltpu.SemaphoreType.DMA((n * PIECES,)),
            pltpu.SemaphoreType.DMA((n * PIECES,)),
        ],
        compiler_params=pltpu.CompilerParams(collective_id=name_id, has_side_effects=True),
    )(block).reshape(slabs * n * rows, columns)


def scatter_kernel(
    n, p_ref, out_ref, stage, from_pair, from_line, pair_send, pair_recv, line_send, line_recv
):
    rank = lax.axis_index("tensor")
    half = n // 2
    high, low = rank // 2, rank % 2
    pair = {"tensor": high * 2 + 1 - low}
    line = [{"tensor": ((high + d) % half) * 2 + low} for d in range(1, half)]
    greet(line + [pair])
    order = list(range(1, half)) + [0]
    pairs = {}
    for d in order:
        pairs[d] = pltpu.make_async_remote_copy(
            src_ref=p_ref.at[((high + d) % half) * 2 + 1 - low],
            dst_ref=from_pair.at[d],
            send_sem=pair_send.at[d],
            recv_sem=pair_recv.at[d],
            device_id=pair,
            device_id_type=MESH_ID,
        )
        pairs[d].start()
    columns = p_ref.shape[2]
    lines = []
    for d in order:
        pairs[d].wait_recv()
        mine = ((high + d) % half) * 2 + low
        if d:
            for c in range(0, columns, 512):
                both = p_ref[mine, :, c : c + 512].astype(jnp.float32) + from_pair[
                    d, :, c : c + 512
                ].astype(jnp.float32)
                stage[d - 1, :, c : c + 512] = both.astype(jnp.bfloat16)
            copy = pltpu.make_async_remote_copy(
                src_ref=stage.at[d - 1],
                dst_ref=from_line.at[d - 1],
                send_sem=line_send.at[d - 1],
                recv_sem=line_recv.at[d - 1],
                device_id=line[d - 1],
                device_id_type=MESH_ID,
            )
            copy.start()
            lines.append(copy)
    for copy in lines:
        copy.wait_recv()
    for c in range(0, columns, 512):
        both = p_ref[rank, :, c : c + 512].astype(jnp.float32) + from_pair[
            0, :, c : c + 512
        ].astype(jnp.float32)
        for d in range(half - 1):
            both = both + from_line[d, :, c : c + 512].astype(jnp.float32)
        out_ref[:, c : c + 512] = both.astype(jnp.bfloat16)
    for d in order:
        pairs[d].wait_send()
    for copy in lines:
        copy.wait_send()


def scatter_sums(partial, n):
    rows, columns = partial.shape[0] // n, partial.shape[1]
    half = n // 2
    return pl.pallas_call(
        functools.partial(scatter_kernel, n),
        out_shape=jax.ShapeDtypeStruct((rows, columns), partial.dtype),
        in_specs=[pl.BlockSpec(memory_space=pltpu.VMEM)],
        out_specs=pl.BlockSpec(memory_space=pltpu.VMEM),
        scratch_shapes=[
            pltpu.VMEM((half - 1, rows, columns), jnp.bfloat16),
            pltpu.VMEM((half, rows, columns), jnp.bfloat16),
            pltpu.VMEM((half - 1, rows, columns), jnp.bfloat16),
            pltpu.SemaphoreType.DMA((half,)),
            pltpu.SemaphoreType.DMA((half,)),
            pltpu.SemaphoreType.DMA((half,)),
            pltpu.SemaphoreType.DMA((half,)),
        ],
        compiler_params=pltpu.CompilerParams(
            collective_id=2, has_side_effects=True, vmem_limit_bytes=32 * 1024 * 1024
        ),
    )(partial.reshape(n, rows, columns))


def row_kinds(section_of_row, section_kind):
    labels = jnp.arange(section_kind.shape[0], dtype=jnp.int32)
    matches = section_of_row[:, None] == labels[None, :]
    return jnp.sum(jnp.where(matches, section_kind[None, :], 0), axis=1)


def apply_rotation(value_matrix, token_places, head_count):
    row_count = value_matrix.shape[0]
    head_dim = value_matrix.shape[1] // head_count
    field_rows = value_matrix.astype(jnp.float32).reshape(row_count, head_count, head_dim)
    frequencies = ROPE_THETA ** (-(jnp.arange(0, head_dim, 2, dtype=jnp.float32) / head_dim))
    angles = token_places.astype(jnp.float32)[:, None] * frequencies[None, :]
    angles = jnp.concatenate([angles, angles], axis=1)
    cosine = jnp.cos(angles)[:, None, :]
    sine_part = jnp.sin(angles)[:, None, :]
    first_half = field_rows[:, :, : head_dim // 2]
    second_half = field_rows[:, :, head_dim // 2 :]
    turned = jnp.concatenate([-second_half, first_half], axis=2)
    rotated = field_rows * cosine + turned * sine_part
    return rotated.reshape(row_count, head_count * head_dim).astype(jnp.bfloat16)


def both_kinds(row_slab, weights, kind_rows):
    first_kind = jnp.dot(row_slab, weights[0], preferred_element_type=jnp.float32)
    second_kind = jnp.dot(row_slab, weights[1], preferred_element_type=jnp.float32)
    return jnp.where(kind_rows[:, None] == 1, second_kind, first_kind)


def project_rows(row_slab, weights, kind_rows):
    return both_kinds(row_slab, weights, kind_rows)


def body(tokens, section_of_row, section_kind, norm_gain, qkv_weight, qkv_bias, out_weight):
    tensor_size = lax.axis_size("tensor")
    tensor_rank = lax.axis_index("tensor")
    seq_rank = lax.axis_index("seq")
    own_rows = tokens.shape[1]
    group_rows = own_rows * tensor_size
    query_span_width = QUERY_HEADS * HEAD_SIZE
    key_value_width = KEY_VALUE_HEADS * HEAD_SIZE
    queries_per_group = QUERY_HEADS // KEY_VALUE_HEADS
    kinds_all = row_kinds(section_of_row, section_kind)
    group_start = seq_rank * group_rows
    kinds_group = lax.dynamic_slice_in_dim(kinds_all, group_start, group_rows)
    own_kinds = lax.dynamic_slice_in_dim(kinds_group, tensor_rank * own_rows, own_rows)
    features = tokens[0].astype(jnp.float32)
    gain_rows = jnp.where(own_kinds[:, None] == 1, norm_gain[1], norm_gain[0]).astype(jnp.float32)
    scaled = lax.rsqrt(jnp.mean(features * features, axis=1, keepdims=True) + NORM_EPSILON)
    normed = (features * scaled * gain_rows).astype(jnp.bfloat16)
    bias_pair = qkv_bias.astype(jnp.float32)
    product = project_rows(
        gather_rows(normed, tensor_size, False, 0), qkv_weight, kinds_group
    )
    column_block = (
        product + jnp.where(kinds_group[:, None] == 1, bias_pair[1], bias_pair[0])
    ).astype(jnp.bfloat16)
    iota_own = jnp.arange(own_rows, dtype=jnp.int32)
    key_places = group_start + tensor_rank * own_rows + iota_own
    row_tile = lax.all_to_all(column_block, "tensor", split_axis=0, concat_axis=1, tiled=True)
    query_matrix = apply_rotation(row_tile[:, :query_span_width], key_places, QUERY_HEADS)
    key_row_values = apply_rotation(
        row_tile[:, query_span_width : query_span_width + key_value_width],
        key_places,
        KEY_VALUE_HEADS,
    )
    value_matrix = row_tile[:, query_span_width + key_value_width :]
    slab = gather_rows(
        jnp.concatenate([key_row_values, value_matrix], axis=1), tensor_size, True, 1
    )
    total_keys = slab.shape[0]
    key_sections = section_of_row
    key_pos = jnp.arange(total_keys, dtype=jnp.int32)
    query_sections = lax.dynamic_slice_in_dim(
        section_of_row, group_start + tensor_rank * own_rows, own_rows
    )
    query_image = own_kinds == 1
    allowed = (key_pos[None, :] <= key_places[:, None]) | (
        key_sections[None, :] == query_sections[:, None]
    ) & query_image[:, None]
    grouped_queries = query_matrix.reshape(own_rows, KEY_VALUE_HEADS, queries_per_group, HEAD_SIZE)
    grouped_queries = grouped_queries.transpose(1, 2, 0, 3).reshape(
        KEY_VALUE_HEADS, queries_per_group * own_rows, HEAD_SIZE
    )
    key_heads = slab[:, :key_value_width].reshape(total_keys, KEY_VALUE_HEADS, HEAD_SIZE)
    value_heads = slab[:, key_value_width:].reshape(total_keys, KEY_VALUE_HEADS, HEAD_SIZE)
    scores = jnp.einsum(
        "gqa,kga->gqk", grouped_queries, key_heads, preferred_element_type=jnp.float32
    ) * (1.0 / math.sqrt(HEAD_SIZE))
    allowed = jnp.broadcast_to(
        allowed[None, None], (1, queries_per_group, own_rows, total_keys)
    ).reshape(1, queries_per_group * own_rows, total_keys)
    scores = jnp.where(allowed, scores, BLOCKED_SCORE)
    peak = jnp.max(scores, axis=2, keepdims=True)
    weights = jnp.where(allowed, jnp.exp(scores - peak), 0.0)
    total = jnp.sum(weights, axis=2)
    summed = jnp.einsum(
        "gqk,kga->gqa",
        weights.astype(jnp.bfloat16),
        value_heads,
        preferred_element_type=jnp.float32,
    )
    attention_result = (summed / total[:, :, None]).astype(jnp.bfloat16)
    attention_result = (
        attention_result.reshape(KEY_VALUE_HEADS, queries_per_group, own_rows, HEAD_SIZE)
        .transpose(2, 0, 1, 3)
        .reshape(own_rows, query_span_width)
    )
    head_block = lax.all_to_all(attention_result, "tensor", split_axis=1, concat_axis=0, tiled=True)
    result = scatter_sums(
        project_rows(head_block, out_weight, kinds_group).astype(jnp.bfloat16), tensor_size
    )
    return result[None]


def solution(mesh):
    placed = (
        P(("groups", "seq"), "tensor", None),
        P("groups"),
        P("groups"),
        P(),
        P(None, None, "tensor"),
        P(None, "tensor"),
        P(None, "tensor", None),
    )
    return jax.shard_map(
        body,
        mesh=mesh,
        in_specs=placed,
        out_specs=P(("groups", "seq"), "tensor", None),
        check_vma=False,
    )
```
